128 devices in a mesh: chan: 64 (over x, y, z_lo, core), quad: 2 (over z_hi).
Axes of the slice: x: 4, y: 4, z: 4 (z_hi: 2, z_lo: 2; z = z_hi * 2 + z_lo), core: 2. Of those that a mesh axis runs over, the one named last changes fastest.
Arguments:
- voltages: float32 [2, 512, 2, 2, 8416], P('quad', 'chan'), may hold values from -6 to 6
- filter_taps: float32 [8, 32], replicated, may hold values from -0.375 to 0.375
- phases: int32 [64, 512, 1024], P('chan', None, 'quad'), may hold values from 0 to 255
Outputs:
- visibilities: float32 [64, 2, 1024, 1024], P('chan', None, 'quad')
- beam_power: float32 [64, 512, 256], P('chan', 'quad')
The draws below stay inside these ranges and needn't reach their ends.
All inputs are finite; a program needn't handle non-finite values.
Results may differ from the reference program's by a relative error of at most 0.0001.
Values sent between devices are 32-bit elements; how exact they have to be, the bound alone decides.
A program may use at most 128 MiB of HBM per device.

```python
import math
import jax
import jax.numpy as jnp
from jax import lax

DISHES = 1024
FINE = 32
TAPS = 8
BEAMS = 512
PHASE_LEVELS = 256
MB = 2
SB = 128
COARSE = 2
CHANNELS = 64
SAMPLES = 8416
N_QUAD = 2


def with_ends(array, rng, low, high):
    dims = array.shape
    spot = [jax.random.randint(jax.random.fold_in(rng, axis), (), 0, dims[axis]) for axis in range(len(dims))]
    array = array.at[tuple(spot)].set(low)
    longest = dims.index(max(dims))
    spot[longest] = (spot[longest] + 1) % dims[longest]
    return array.at[tuple(spot)].set(high)


def steps_of(rng, shape, split, smallest, largest):
    gain = 1.0
    for position, blocks in split:
        steps = jax.random.uniform(jax.random.fold_in(jax.random.fold_in(rng, 6), position), (blocks,), jnp.float32, smallest / len(split), largest / len(split))
        gain = gain * jnp.repeat(jnp.exp(steps), shape[position] // blocks).reshape((-1,) + (1,) * (len(shape) - 1 - position))
    return gain


def centred(stream_key, dims, scale, limit, split=(), kind=jnp.bfloat16):
    drawn = scale * jax.random.normal(stream_key, dims, jnp.float32)
    if split:
        drawn = drawn * steps_of(stream_key, dims, split, -0.22, 0.18)
    return jnp.clip(drawn, -limit, limit).astype(kind)


def setup_inputs(seed: int = 0) -> dict:
    splits = jax.random.split(jax.random.key(seed), 4)
    voltages = centred(splits[0], (N_QUAD, DISHES // N_QUAD, COARSE, 2, SAMPLES), 1.0, 6.0, ((0, 2), (1, 64)), jnp.float32)
    filter_taps = centred(splits[1], (TAPS, FINE), (TAPS * FINE) ** -0.5, 0.375, (), jnp.float32)
    phases = with_ends(jax.random.randint(splits[2], (CHANNELS, BEAMS, DISHES), 0, PHASE_LEVELS), jax.random.fold_in(splits[2], 1), 0, PHASE_LEVELS - 1).astype(jnp.int32)
    return {"voltages": voltages, "filter_taps": filter_taps, "phases": phases}


highest = lax.Precision.HIGHEST


def dft_matrix():
    index_n = jnp.arange(FINE, dtype=jnp.int32)
    product = (index_n[:, None] * index_n[None, :]) % FINE
    angles = product.astype(jnp.float32) * (2.0 * math.pi / FINE)
    cosine = jnp.cos(angles)
    sine = jnp.sin(angles)
    return jnp.stack([jnp.stack([cosine, sine]), jnp.stack([-sine, cosine])])


def reference(voltages, filter_taps, phases):
    spectra_total = MB * SB
    frames = voltages.reshape(DISHES, COARSE, 2, spectra_total + TAPS - 1, FINE)
    filtered = jnp.zeros((DISHES, COARSE, 2, spectra_total, FINE), jnp.float32)
    for tap_index in range(TAPS):
        filtered = filtered + filter_taps[tap_index] * frames[:, :, :, tap_index:tap_index + spectra_total, :]
    spectra = jnp.einsum("dbisn,jink->bkdjs", filtered, dft_matrix(), precision=highest)
    spectra = spectra.reshape(CHANNELS, DISHES, 2, spectra_total)

    def per_channel(operands):
        channel_spec, channel_phase = operands
        left_side = channel_spec.reshape(DISHES, 2 * spectra_total)
        swapped = jnp.concatenate([-channel_spec[:, 1], channel_spec[:, 0]], axis=-1)
        right_side = jnp.stack([left_side, swapped])
        visible = jnp.einsum("rk,vqk->vrq", left_side, right_side, precision=highest) / spectra_total
        steer_angle = channel_phase.astype(jnp.float32) * (2.0 * math.pi / PHASE_LEVELS)
        cosine = jnp.cos(steer_angle)
        sine = jnp.sin(steer_angle)
        gains = jnp.stack([jnp.stack([cosine, sine], -1), jnp.stack([-sine, cosine], -1)])
        beams = jnp.einsum("vbri,ris->vbs", gains, channel_spec, precision=highest)
        power_out = (beams[0] * beams[0] + beams[1] * beams[1]) / DISHES
        return visible, power_out

    visibilities, beam_power = lax.map(per_channel, (spectra, phases))
    return visibilities, beam_power
```

```python
import functools
import math

import jax
import jax.numpy as jnp
import numpy as np
from jax import lax
from jax.experimental import pallas as pl
from jax.experimental.pallas import tpu as pltpu
from jax.sharding import PartitionSpec as P

MESH = pl.DeviceIdType.MESH
F32 = jnp.float32
BF16 = jnp.bfloat16
VMEM = pltpu.VMEM
DMA = pltpu.SemaphoreType.DMA

DISHES = 1024
HALF = 512
FINE = 32
TAPS = 8
LEVELS = 256
SPECTRA = 256
PEERS = 128
BEAMS = 256
NT = (((1,), (1,)), ((), ()))


def sine_terms():
    nodes = 64.0 * np.cos((np.arange(400) + 0.5) * np.pi / 800)
    basis = np.stack([nodes ** (2 * i + 1) / 64.0 ** (2 * i + 1) for i in range(6)], 1)
    fit = np.linalg.lstsq(basis, np.sin(np.pi * nodes / 128), rcond=None)[0]
    return [float(fit[i] / 64.0 ** (2 * i + 1)) for i in range(6)]


SINE = sine_terms()


def split(value):
    high = value.astype(BF16)
    return high, (value - high.astype(F32)).astype(BF16)


def steer(level):
    wrapped = (level + 128) % LEVELS - 128
    unit = (64 - jnp.abs(wrapped)).astype(F32)
    square = unit * unit
    total = jnp.full_like(square, SINE[5])
    for term in SINE[4::-1]:
        total = total * square + term
    return total * unit


def peer(step):
    chan = lax.axis_index("chan")
    quad = lax.axis_index("quad")
    me = chan * 2 + quad
    turn = lax.rem(step * (2 * me + 1), PEERS)
    z = lax.rem(quad * 2 + lax.rem(chan // 2, 2) + lax.rem(turn, 4), 4)
    x = lax.rem(chan // 16 + lax.rem(turn // 4, 4), 4)
    y = lax.rem(lax.rem(chan // 4, 4) + lax.rem(turn // 16, 4), 4)
    core = lax.rem(lax.rem(chan, 2) + turn // 64, 2)
    return x * 16 + y * 4 + lax.rem(z, 2) * 2 + core, z // 2


def transform_table():
    row = lax.broadcasted_iota(jnp.int32, (FINE, 128), 0)
    col = lax.broadcasted_iota(jnp.int32, (FINE, 128), 1) % FINE
    angle = ((row * col) % FINE) * (LEVELS // FINE)
    return steer(angle), steer(angle - 64)


def filter_rows(taps):
    wide = jnp.concatenate([taps] * 4, axis=1)
    tap = lax.broadcasted_iota(jnp.int32, (TAPS, 128), 0)
    group = lax.broadcasted_iota(jnp.int32, (TAPS, 128), 1) // FINE
    rows = []
    for f in range(4):
        rows.append(
            [
                jnp.sum(jnp.where(tap == 4 * a + group - f, wide, 0.0), axis=0, keepdims=True)
                for a in range(3)
            ]
        )
    return rows


def spectra_kernel(volt_hbm, taps_ref, phase_hbm, got_ref, gains_hi, gains_lo,
                   volt, lines, bank, send, phase_own, phase_far,
                   load_sem, send_sem, recv_sem, phase_sems):
    chan = lax.axis_index("chan")
    quad = lax.axis_index("quad")

    load = pltpu.make_async_copy(volt_hbm.at[0], volt, load_sem)
    load.start()
    own = pltpu.make_async_copy(phase_hbm.at[0, pl.ds(quad * BEAMS, BEAMS)], phase_own, phase_sems.at[2])
    own.start()

    barrier = pltpu.get_barrier_semaphore()

    def greet(step, carry):
        pl.semaphore_signal(barrier, inc=1, device_id=peer(step), device_id_type=MESH)
        return carry

    lax.fori_loop(1, PEERS, greet, 0)
    pl.semaphore_wait(barrier, PEERS - 1)

    far = pltpu.make_async_remote_copy(
        src_ref=phase_hbm.at[0, pl.ds((1 - quad) * BEAMS, BEAMS)], dst_ref=phase_far,
        send_sem=phase_sems.at[0], recv_sem=phase_sems.at[1],
        device_id=(chan, 1 - quad), device_id_type=MESH)
    far.start()

    cosine, sine = transform_table()
    taps = filter_rows(taps_ref[...])
    for g in range(2):
        for r in range(2):
            for f in range(2):
                tables = (cosine, sine) if r == 0 else (-sine, cosine)
                at = ((g * 2 + r) * 2 + f) * FINE
                for i in range(2):
                    for a in range(3):
                        high, low = split(tables[i] * taps[2 * g + f][a])
                        col = (i * 3 + a) * 128
                        bank[at:at + FINE, col:col + 128] = high
                        bank[at:at + FINE, 768 + col:768 + col + 128] = high
                        bank[at:at + FINE, 1536 + col:1536 + col + 128] = low

    load.wait()
    for d in range(8):
        for b in range(2):
            for r in range(2):
                lines[d, b, r, 0:64, :] = volt[d, b, r, 0:8192].reshape(64, 128)
                lines[d, b, r, 64:72, :] = jnp.zeros((8, 128), F32)
                lines[d, b, r, 64:65, :] = volt[d, b, r, 8192:8320].reshape(1, 128)
                lines[d, b, r, 65:66, 0:96] = volt[d, b, r, 8320:8416].reshape(1, 96)

    lane = lax.broadcasted_iota(jnp.int32, (FINE, 128), 1)
    for b in range(2):
        for h in range(2):
            high_parts = []
            low_parts = []
            for r in range(2):
                for a in range(3):
                    block = jnp.concatenate([lines[4 * h + d, b, r, a:a + 64, :] for d in range(4)], axis=0)
                    high, low = split(block)
                    high_parts.append(high)
                    low_parts.append(low)
            right = jnp.concatenate(high_parts + low_parts + high_parts, axis=1)
            out = lax.dot_general(bank[...], right, NT, preferred_element_type=F32)
            for g in range(2):
                for r in range(2):
                    at = (g * 2 + r) * 2 * FINE
                    for p in range(2):
                        first = out[at:at + FINE, 128 * p:128 * p + 128]
                        second = out[at + FINE:at + 2 * FINE, 128 * p:128 * p + 128]
                        even = jnp.where(lane < 64, first, pltpu.roll(second, 64, 1))
                        odd = jnp.where(lane < 64, pltpu.roll(first, 64, 1), second)
                        part = 2 * g + r
                        send[part, pl.ds(b * 256 + 4 * h + 2 * p, FINE, stride=8), :] = even
                        send[part, pl.ds(b * 256 + 4 * h + 2 * p + 1, FINE, stride=8), :] = odd

    mine = pl.ds(pl.multiple_of(quad * HALF + chan * 8, 8), 8)
    for g in range(2):
        parts = pl.ds(2 * g, 2)

        def push(step, carry):
            to_chan, to_quad = peer(step)
            pltpu.make_async_remote_copy(
                src_ref=send.at[parts, pl.ds(pl.multiple_of(to_chan * 8, 8), 8)], dst_ref=got_ref.at[parts, mine],
                send_sem=send_sem.at[g], recv_sem=recv_sem.at[g],
                device_id=(to_chan, to_quad), device_id_type=MESH).start()
            return carry

        lax.fori_loop(1, PEERS, push, 0)
    for part in range(4):
        got_ref[part, mine, :] = send[part, pl.ds(pl.multiple_of(chan * 8, 8), 8), :]

    def gains(source, half):
        for start in range(0, BEAMS, 32):
            level = source[start:start + 32, :]
            for i in range(2):
                high, low = split(steer(level - 64 * i))
                cols = pl.ds(pl.multiple_of(i * DISHES + half * HALF, HALF), HALF)
                gains_hi[start:start + 32, cols] = high
                gains_lo[start:start + 32, cols] = low

    own.wait()
    gains(phase_own, quad)
    far.wait_recv()
    gains(phase_far, 1 - quad)

    for g in range(2):
        whole = got_ref.at[pl.ds(2 * g, 2), pl.ds(0, (PEERS - 1) * 8)]
        pltpu.make_async_copy(whole, whole, recv_sem.at[g]).wait()
        pltpu.make_async_copy(whole, whole, send_sem.at[g]).wait()
    far.wait_send()


def turned(block):
    parts = []
    for g in range(2):
        parts += [block[:, g * 256 + 128:g * 256 + 256], -block[:, g * 256:g * 256 + 128]]
    return jnp.concatenate(parts, axis=1)


def joined(ref, rows):
    return jnp.concatenate([ref[part, rows, :] for part in range(4)], axis=1)


def product_kernel(got_ref, gains_hi, gains_lo, vis_ref, power_ref, left, right):
    quad = lax.axis_index("quad")

    @pl.when(pl.program_id(0) == 0)
    def _():
        for start in range(0, DISHES, 128):
            rows = slice(start, start + 128)
            high, low = split(joined(got_ref, rows))
            right[rows, 0:512] = high
            right[rows, 512:1024] = low
            right[rows, 1024:1536] = high
        for start in range(0, HALF, 128):
            rows = pl.ds(pl.multiple_of(quad * HALF + start, 128), 128)
            block = joined(got_ref, rows) * (1.0 / SPECTRA)
            high, low = split(block)
            left[start:start + 128, 0:512] = high
            left[start:start + 128, 512:1024] = high
            left[start:start + 128, 1024:1536] = low
            high, low = turned(high), turned(low)
            left[HALF + start:HALF + start + 128, 0:512] = high
            left[HALF + start:HALF + start + 128, 512:1024] = high
            left[HALF + start:HALF + start + 128, 1024:1536] = low

    cols = pl.ds(pl.multiple_of(pl.program_id(0) * 256, 256), 256)
    out = lax.dot_general(left[...], right[cols, :], NT, preferred_element_type=F32)
    vis_ref[0, 0] = out[0:HALF]
    vis_ref[0, 1] = out[HALF:]

    @pl.when(pl.program_id(0) == 0)
    def _():
        high = right[:, 0:512]
        low = right[:, 512:1024]
        both_high = jnp.concatenate([high, turned(high)], axis=0)
        both_low = jnp.concatenate([low, turned(low)], axis=0)
        beams = jnp.dot(gains_hi[...], both_high, preferred_element_type=F32)
        beams += jnp.dot(gains_hi[...], both_low, preferred_element_type=F32)
        beams += jnp.dot(gains_lo[...], both_high, preferred_element_type=F32)
        beams = beams * beams
        power = jnp.concatenate(
            [beams[:, 0:128] + beams[:, 128:256], beams[:, 256:384] + beams[:, 384:512]], axis=1
        ) * (1.0 / DISHES)
        source = lax.broadcasted_iota(jnp.int32, (SPECTRA, SPECTRA), 0)
        target = lax.broadcasted_iota(jnp.int32, (SPECTRA, SPECTRA), 1)
        order = (4 * (source % 64) + source // 64 == target).astype(BF16)
        high = power.astype(BF16)
        rest = power - high.astype(F32)
        middle, low = split(rest)
        power_ref[0] = (
            jnp.dot(high, order, preferred_element_type=F32)
            + jnp.dot(middle, order, preferred_element_type=F32)
            + jnp.dot(low, order, preferred_element_type=F32)
        )


def per_device(voltages, filter_taps, phases):
    any_space = pl.BlockSpec(memory_space=pl.ANY)
    vmem_space = pl.BlockSpec(memory_space=VMEM)
    got, gains_hi, gains_lo = pl.pallas_call(
        spectra_kernel,
        name="spectra",
        out_shape=(
            jax.ShapeDtypeStruct((4, DISHES, 128), F32),
            jax.ShapeDtypeStruct((BEAMS, 2 * DISHES), BF16),
            jax.ShapeDtypeStruct((BEAMS, 2 * DISHES), BF16),
        ),
        in_specs=[any_space, vmem_space, any_space],
        out_specs=(vmem_space, vmem_space, vmem_space),
        scratch_shapes=[
            VMEM((8, 2, 2, 8416), F32),
            VMEM((8, 2, 2, 72, 128), F32),
            VMEM((256, 2304), BF16),
            VMEM((4, 512, 128), F32),
            VMEM((BEAMS, HALF), jnp.int32),
            VMEM((BEAMS, HALF), jnp.int32),
            DMA,
            DMA((2,)),
            DMA((2,)),
            DMA((3,)),
        ],
        compiler_params=pltpu.CompilerParams(
            collective_id=0, has_side_effects=True, vmem_limit_bytes=24 * 2**20
        ),
    )(voltages, filter_taps, phases)
    return pl.pallas_call(
        product_kernel,
        name="products",
        grid=(4,),
        out_shape=(
            jax.ShapeDtypeStruct((1, 2, HALF, DISHES), F32),
            jax.ShapeDtypeStruct((1, BEAMS, SPECTRA), F32),
        ),
        in_specs=[vmem_space, vmem_space, vmem_space],
        out_specs=(
            pl.BlockSpec((1, 2, HALF, 256), lambda i: (0, 0, 0, i)),
            pl.BlockSpec((1, BEAMS, SPECTRA), lambda i: (0, 0, 0)),
        ),
        scratch_shapes=[VMEM((DISHES, 1536), BF16), VMEM((DISHES, 1536), BF16)],
        compiler_params=pltpu.CompilerParams(vmem_limit_bytes=32 * 2**20),
    )(got, gains_hi, gains_lo)


def solution(mesh):
    return jax.shard_map(
        per_device,
        mesh=mesh,
        in_specs=(P("quad", "chan", None, None, None), P(), P("chan", None, "quad")),
        out_specs=(P("chan", None, "quad", None), P("chan", "quad", None)),
        check_vma=False,
    )
```

```python
import functools
import math

import jax
import jax.numpy as jnp
import numpy as np
from jax import lax
from jax.experimental import pallas as pl
from jax.experimental.pallas import tpu as pltpu
from jax.sharding import PartitionSpec as P

MESH = pl.DeviceIdType.MESH
F32 = jnp.float32
BF16 = jnp.bfloat16
VMEM = pltpu.VMEM
DMA = pltpu.SemaphoreType.DMA

DISHES = 1024
HALF = 512
FINE = 32
TAPS = 8
LEVELS = 256
SPECTRA = 256
PEERS = 128
BEAMS = 256
NT = (((1,), (1,)), ((), ()))


def sine_terms():
    nodes = 64.0 * np.cos((np.arange(400) + 0.5) * np.pi / 800)
    basis = np.stack([nodes ** (2 * i + 1) / 64.0 ** (2 * i + 1) for i in range(6)], 1)
    fit = np.linalg.lstsq(basis, np.sin(np.pi * nodes / 128), rcond=None)[0]
    return [float(fit[i] / 64.0 ** (2 * i + 1)) for i in range(6)]


SINE = sine_terms()


def split(value):
    high = value.astype(BF16)
    return high, (value - high.astype(F32)).astype(BF16)


def steer(level):
    wrapped = (level + 128) % LEVELS - 128
    unit = (64 - jnp.abs(wrapped)).astype(F32)
    square = unit * unit
    total = jnp.full_like(square, SINE[5])
    for term in SINE[4::-1]:
        total = total * square + term
    return total * unit


def each_peer(visit, after):
    chan = lax.axis_index("chan")
    quad = lax.axis_index("quad")
    x, y, z, core = chan // 16, (chan // 4) % 4, quad * 2 + (chan // 2) % 2, chan % 2
    ends = []
    for dc in range(2):
        for dz in (2, 1, 3, 0):
            there = (z + dz) % 4
            ends.append((dz + dc, (there % 2) * 2 + (core + dc) % 2, there // 2))

    def step(t, here):
        column = ((x + t % 4) % 4) * 16 + ((y + t // 4) % 4) * 4
        for shift, low, there in ends:
            if shift or not here:
                visit(t, column + low, there)

    step(0, True)
    after(0)

    def body(t, carry):
        step(t, False)
        after(t)
        return carry

    lax.fori_loop(1, 16, body, 0)


def transform_table():
    row = lax.broadcasted_iota(jnp.int32, (FINE, 128), 0)
    col = lax.broadcasted_iota(jnp.int32, (FINE, 128), 1) % FINE
    angle = ((row * col) % FINE) * (LEVELS // FINE)
    return steer(angle), steer(angle - 64)


def filter_rows(taps):
    wide = jnp.concatenate([taps] * 4, axis=1)
    tap = lax.broadcasted_iota(jnp.int32, (TAPS, 128), 0)
    group = lax.broadcasted_iota(jnp.int32, (TAPS, 128), 1) // FINE
    rows = []
    for f in range(4):
        rows.append(
            [
                jnp.sum(jnp.where(tap == 4 * a + group - f, wide, 0.0), axis=0, keepdims=True)
                for a in range(3)
            ]
        )
    return rows


def spectra_kernel(volt_hbm, taps_hbm, phase_hbm, sums_ref, left, right, own_hi, own_lo, far_hi, far_lo, power_ref,
                   volt, taps_ref, lines, bank, send, got, phase_own, phase_far,
                   load_sem, taps_sem, send_sem, recv_sem, own_sem, far_send, far_recv):
    chan = lax.axis_index("chan")
    quad = lax.axis_index("quad")

    load = pltpu.make_async_copy(volt_hbm.at[0], volt, load_sem)
    load.start()
    load_taps = pltpu.make_async_copy(taps_hbm, taps_ref, taps_sem)
    load_taps.start()
    own = pltpu.make_async_copy(phase_hbm.at[0, pl.ds(quad * BEAMS, BEAMS)], phase_own, own_sem)
    own.start()

    barrier = pltpu.get_barrier_semaphore()

    def greet(step, to_chan, to_quad):
        pl.semaphore_signal(barrier, inc=1, device_id=(to_chan, to_quad), device_id_type=MESH)

    each_peer(greet, lambda step: None)

    cosine, sine = transform_table()
    load_taps.wait()
    taps = filter_rows(taps_ref[...])
    for g in range(2):
        for r in range(2):
            for f in range(2):
                tables = (cosine, sine) if r == 0 else (-sine, cosine)
                at = ((g * 2 + r) * 2 + f) * FINE
                for i in range(2):
                    for a in range(3):
                        high, low = split(tables[i] * taps[2 * g + f][a])
                        col = (i * 3 + a) * 128
                        bank[at:at + FINE, col:col + 128] = high
                        bank[at:at + FINE, 768 + col:768 + col + 128] = high
                        bank[at:at + FINE, 1536 + col:1536 + col + 128] = low

    load.wait()
    for d in range(8):
        for b in range(2):
            for r in range(2):
                lines[d, b, r, 0:64, :] = volt[d, b, r, 0:8192].reshape(64, 128)
                lines[d, b, r, 64:72, :] = jnp.zeros((8, 128), F32)
                lines[d, b, r, 64:65, :] = volt[d, b, r, 8192:8320].reshape(1, 128)
                lines[d, b, r, 65:66, 0:96] = volt[d, b, r, 8320:8416].reshape(1, 96)

    lane = lax.broadcasted_iota(jnp.int32, (FINE, 128), 1)
    for b in range(2):
        for h in range(2):
            high_parts = []
            low_parts = []
            for r in range(2):
                for a in range(3):
                    block = jnp.concatenate([lines[4 * h + d, b, r, a:a + 64, :] for d in range(4)], axis=0)
                    high, low = split(block)
                    high_parts.append(high)
                    low_parts.append(low)
            window = jnp.concatenate(high_parts + low_parts + high_parts, axis=1)
            out = lax.dot_general(bank[...], window, NT, preferred_element_type=F32)
            for g in range(2):
                for r in range(2):
                    part = 2 * g + r
                    for p in range(2):
                        cols = slice(128 * p, 128 * p + 128)
                        first = out[part * 64:part * 64 + FINE, cols]
                        second = out[part * 64 + FINE:part * 64 + 2 * FINE, cols]
                        even = jnp.where(lane < 64, first, pltpu.roll(second, 64, 1))
                        odd = jnp.where(lane < 64, pltpu.roll(first, 64, 1), second)
                        at = b * 1024 + part * 8 + 4 * h + 2 * p
                        send[pl.ds(at, FINE, stride=32), :] = even
                        send[pl.ds(at + 1, FINE, stride=32), :] = odd

    slot = quad * 64 + chan

    def far(piece):
        return pltpu.make_async_remote_copy(
            src_ref=phase_hbm.at[0, pl.ds(pl.multiple_of((1 - quad) * BEAMS + piece * 8, 8), 8)],
            dst_ref=phase_far.at[pl.ds(pl.multiple_of(piece * 8, 8), 8)],
            send_sem=far_send, recv_sem=far_recv,
            device_id=(chan, 1 - quad), device_id_type=MESH)

    def far_all(sem):
        pltpu.make_async_copy(phase_far, phase_far, sem).wait()

    pl.semaphore_wait(barrier, PEERS - 1)
    for g in range(2):

        def push(step, to_chan, to_quad):
            pltpu.make_async_remote_copy(
                src_ref=send.at[pl.ds(pl.multiple_of(to_chan * 32 + 16 * g, 16), 16)],
                dst_ref=got.at[slot, pl.ds(16 * g, 16)],
                send_sem=send_sem.at[g], recv_sem=recv_sem.at[g],
                device_id=(to_chan, to_quad), device_id_type=MESH).start()

        each_peer(push, lambda step: far(16 * g + step).start())
    got[slot] = send[pl.ds(pl.multiple_of(chan * 32, 32), 32), :]

    own.wait()
    gains(phase_own, own_hi, own_lo)
    arrived(got, recv_sem.at[0], 0)
    prepare(got, 0, quad, left, right)

    def product(tile, carry):
        cols = pl.ds(pl.multiple_of(tile * 256, 256), 256)
        sums_ref[:, cols] = lax.dot_general(left[...], right[cols, :], NT, preferred_element_type=F32)
        return carry

    lax.fori_loop(0, 4, product, 0)
    far_all(far_recv)
    gains(phase_far, far_hi, far_lo)
    power_ref[...] = powered(quad, own_hi, own_lo, far_hi, far_lo, right)

    arrived(got, recv_sem.at[1], 1)
    prepare(got, 1, quad, left, right)
    for g in range(2):
        arrived(got, send_sem.at[g], g)
    far_all(far_send)


def gains(source, high_ref, low_ref):
    for start in range(0, source.shape[0], 32):
        level = source[start:start + 32, :]
        for i in range(2):
            high, low = split(steer(level - 64 * i))
            high_ref[start:start + 32, i * HALF:i * HALF + HALF] = high
            low_ref[start:start + 32, i * HALF:i * HALF + HALF] = low


def arrived(got, sem, g):
    whole = got.at[pl.ds(0, PEERS - 1), pl.ds(16 * g, 16)]
    pltpu.make_async_copy(whole, whole, sem).wait()


def turned(block):
    return jnp.concatenate([block[:, 128:256], -block[:, 0:128]], axis=1)


def prepare(got, g, quad, left, right):
    for start in range(0, DISHES, 128):
        rows = slice(start, start + 128)
        block = got[start // 8:start // 8 + 16, 16 * g:16 * g + 16, :]
        high, low = split(
            jnp.concatenate([block[:, 0:8].reshape(128, 128), block[:, 8:16].reshape(128, 128)], axis=1))
        right[rows, 0:256] = high
        right[rows, 256:512] = low
        right[rows, 512:768] = high
    for start in range(0, HALF, 128):
        rows = pl.ds(pl.multiple_of(quad * HALF + start, 128), 128)
        high = right[rows, 0:256] * (1.0 / SPECTRA)
        low = right[rows, 256:512] * (1.0 / SPECTRA)
        left[start:start + 128, 0:256] = high
        left[start:start + 128, 256:512] = high
        left[start:start + 128, 512:768] = low
        high, low = turned(high), turned(low)
        left[HALF + start:HALF + start + 128, 0:256] = high
        left[HALF + start:HALF + start + 128, 256:512] = high
        left[HALF + start:HALF + start + 128, 512:768] = low


def steered(gains_hi, gains_lo, right, rows):
    high = right[rows, 0:256]
    low = right[rows, 256:512]
    both_high = jnp.concatenate([high, turned(high)], axis=0)
    both_low = jnp.concatenate([low, turned(low)], axis=0)
    beams = jnp.dot(gains_hi[...], both_high, preferred_element_type=F32)
    beams += jnp.dot(gains_hi[...], both_low, preferred_element_type=F32)
    beams += jnp.dot(gains_lo[...], both_high, preferred_element_type=F32)
    return beams


def powered(quad, own_hi, own_lo, far_hi, far_lo, right):
    near = pl.ds(pl.multiple_of(quad * HALF, HALF), HALF)
    other = pl.ds(pl.multiple_of((1 - quad) * HALF, HALF), HALF)
    beams = steered(own_hi, own_lo, right, near) + steered(far_hi, far_lo, right, other)
    beams = beams * beams
    return (beams[:, 0:128] + beams[:, 128:256]) * (1.0 / DISHES)


def finish_kernel(sums_ref, left, right, own_hi, own_lo, far_hi, far_lo, first_power, vis_hbm, power_hbm,
                  vis_ref, power_ref, vis_sem, power_sem):
    quad = lax.axis_index("quad")
    copies = []
    for tile in range(4):
        cols = pl.ds(tile * 256, 256)
        vis_ref[tile] = sums_ref[:, cols] + lax.dot_general(left[...], right[cols, :], NT, preferred_element_type=F32)
        for i in range(2):
            copies.append(pltpu.make_async_copy(
                vis_ref.at[tile, pl.ds(i * HALF, HALF)], vis_hbm.at[0, i, :, cols], vis_sem.at[2 * tile + i]))
            copies[-1].start()

    power = jnp.concatenate([first_power[...], powered(quad, own_hi, own_lo, far_hi, far_lo, right)], axis=1)
    source = lax.broadcasted_iota(jnp.int32, (SPECTRA, SPECTRA), 0)
    target = lax.broadcasted_iota(jnp.int32, (SPECTRA, SPECTRA), 1)
    order = (4 * (source % 64) + source // 64 == target).astype(BF16)
    high = power.astype(BF16)
    middle, low = split(power - high.astype(F32))
    power_ref[...] = (
        jnp.dot(high, order, preferred_element_type=F32)
        + jnp.dot(middle, order, preferred_element_type=F32)
        + jnp.dot(low, order, preferred_element_type=F32)
    )
    copy = pltpu.make_async_copy(power_ref, power_hbm.at[0], power_sem)
    copy.start()
    copy.wait()
    for copy in copies:
        copy.wait()


def per_device(voltages, filter_taps, phases):
    hbm_space = pl.BlockSpec(memory_space=pltpu.HBM)
    vmem_space = pl.BlockSpec(memory_space=VMEM)
    made = pl.pallas_call(
        spectra_kernel,
        name="spectra",
        out_shape=(
            jax.ShapeDtypeStruct((DISHES, DISHES), F32),
            jax.ShapeDtypeStruct((DISHES, 768), BF16),
            jax.ShapeDtypeStruct((DISHES, 768), BF16),
            jax.ShapeDtypeStruct((BEAMS, DISHES), BF16),
            jax.ShapeDtypeStruct((BEAMS, DISHES), BF16),
            jax.ShapeDtypeStruct((BEAMS, DISHES), BF16),
            jax.ShapeDtypeStruct((BEAMS, DISHES), BF16),
            jax.ShapeDtypeStruct((BEAMS, 128), F32),
        ),
        in_specs=[hbm_space] * 3,
        out_specs=(vmem_space,) * 8,
        scratch_shapes=[
            VMEM((8, 2, 2, 8416), F32),
            VMEM((TAPS, FINE), F32),
            VMEM((8, 2, 2, 72, 128), F32),
            VMEM((256, 2304), BF16),
            VMEM((2048, 128), F32),
            VMEM((PEERS, 32, 128), F32),
            VMEM((BEAMS, HALF), jnp.int32),
            VMEM((BEAMS, HALF), jnp.int32),
            DMA,
            DMA,
            DMA((2,)),
            DMA((2,)),
            DMA,
            DMA,
            DMA,
        ],
        compiler_params=pltpu.CompilerParams(
            collective_id=0, has_side_effects=True, vmem_limit_bytes=28 * 2**20
        ),
    )(*[pltpu.with_memory_space_constraint(x, pltpu.HBM) for x in (voltages, filter_taps, phases)])
    return pl.pallas_call(
        finish_kernel,
        name="finish",
        out_shape=(
            jax.ShapeDtypeStruct((1, 2, HALF, DISHES), F32),
            jax.ShapeDtypeStruct((1, BEAMS, SPECTRA), F32),
        ),
        in_specs=[vmem_space] * 8,
        out_specs=(hbm_space, hbm_space),
        scratch_shapes=[VMEM((4, DISHES, 256), F32), VMEM((BEAMS, SPECTRA), F32), DMA((8,)), DMA],
        compiler_params=pltpu.CompilerParams(vmem_limit_bytes=16 * 2**20),
    )(*made)


def solution(mesh):
    return jax.shard_map(
        per_device,
        mesh=mesh,
        in_specs=(P("quad", "chan", None, None, None), P(), P("chan", None, "quad")),
        out_specs=(P("chan", None, "quad", None), P("chan", "quad", None)),
        check_vma=False,
    )
```

```python
import functools
import math

import jax
import jax.numpy as jnp
import numpy as np
from jax import lax
from jax.experimental import pallas as pl
from jax.experimental.pallas import tpu as pltpu
from jax.sharding import PartitionSpec as P

MESH = pl.DeviceIdType.MESH
F32 = jnp.float32
BF16 = jnp.bfloat16
VMEM = pltpu.VMEM
DMA = pltpu.SemaphoreType.DMA

DISHES = 1024
HALF = 512
FINE = 32
TAPS = 8
LEVELS = 256
SPECTRA = 256
PEERS = 128
BEAMS = 256
LOTS = (0, 128, 256)
CHUNKS = ((0, 3), (3, 4))
NT = (((1,), (1,)), ((), ()))


def sine_terms():
    nodes = 64.0 * np.cos((np.arange(400) + 0.5) * np.pi / 800)
    basis = np.stack([nodes ** (2 * i + 1) / 64.0 ** (2 * i + 1) for i in range(6)], 1)
    fit = np.linalg.lstsq(basis, np.sin(np.pi * nodes / 128), rcond=None)[0]
    return [float(fit[i] / 64.0 ** (2 * i + 1)) for i in range(6)]


SINE = sine_terms()


def split(value):
    high = value.astype(BF16)
    return high, (value - high.astype(F32)).astype(BF16)


def steer(level):
    wrapped = (level + 128) % LEVELS - 128
    unit = (64 - jnp.abs(wrapped)).astype(F32)
    square = unit * unit
    total = jnp.full_like(square, SINE[5])
    for term in SINE[4::-1]:
        total = total * square + term
    return total * unit


def each_peer(visit, after):
    chan = lax.axis_index("chan")
    quad = lax.axis_index("quad")
    x, y, z, core = chan // 16, (chan // 4) % 4, quad * 2 + (chan // 2) % 2, chan % 2
    ends = []
    for dc in range(2):
        for dz in (2, 1, 3, 0):
            there = (z + dz) % 4
            ends.append((dz + dc, (there % 2) * 2 + (core + dc) % 2, there // 2))

    def step(t, here):
        column = ((x + t % 4) % 4) * 16 + ((y + t // 4) % 4) * 4
        for shift, low, there in ends:
            if shift or not here:
                visit(t, column + low, there)

    step(0, True)
    after(0)

    def body(t, carry):
        step(t, False)
        after(t)
        return carry

    lax.fori_loop(1, 16, body, 0)


def transform_table():
    row = lax.broadcasted_iota(jnp.int32, (FINE, 128), 0)
    col = lax.broadcasted_iota(jnp.int32, (FINE, 128), 1) % FINE
    angle = ((row * col) % FINE) * (LEVELS // FINE)
    return steer(angle), steer(angle - 64)


def filter_rows(taps):
    wide = jnp.concatenate([taps] * 4, axis=1)
    tap = lax.broadcasted_iota(jnp.int32, (TAPS, 128), 0)
    group = lax.broadcasted_iota(jnp.int32, (TAPS, 128), 1) // FINE
    rows = []
    for f in range(4):
        rows.append(
            [
                jnp.sum(jnp.where(tap == 4 * a + group - f, wide, 0.0), axis=0, keepdims=True)
                for a in range(3)
            ]
        )
    return rows


def spectra_kernel(volt_hbm, taps_hbm, phase_hbm, sums_ref, left, both_all, own_hi, own_lo, far_hi, far_lo, power_ref,
                   volt, taps_ref, lines, bank, send, got, first_all, first_left, second_left, phase_own, phase_far,
                   load_sem, taps_sem, send_sem, recv_sem, own_sem, far_send, far_recv):
    chan = lax.axis_index("chan")
    quad = lax.axis_index("quad")

    load = pltpu.make_async_copy(volt_hbm.at[0], volt, load_sem)
    load.start()
    load_taps = pltpu.make_async_copy(taps_hbm, taps_ref, taps_sem)
    load_taps.start()
    own = pltpu.make_async_copy(phase_hbm.at[0, pl.ds(quad * BEAMS, BEAMS)], phase_own, own_sem)
    own.start()

    barrier = pltpu.get_barrier_semaphore()

    def greet(step, to_chan, to_quad):
        pl.semaphore_signal(barrier, inc=1, device_id=(to_chan, to_quad), device_id_type=MESH)

    each_peer(greet, lambda step: None)

    cosine, sine = transform_table()
    load_taps.wait()
    taps = filter_rows(taps_ref[...])
    for f in range(4):
        for r in range(2):
            tables = (cosine, sine) if r == 0 else (-sine, cosine)
            at = (f * 2 + r) * FINE
            for i in range(2):
                for a in range(3):
                    high, low = split(tables[i] * taps[f][a])
                    col = (i * 3 + a) * 128
                    bank[at:at + FINE, col:col + 128] = high
                    bank[at:at + FINE, 768 + col:768 + col + 128] = high
                    bank[at:at + FINE, 1536 + col:1536 + col + 128] = low

    load.wait()
    for d in range(8):
        for b in range(2):
            for r in range(2):
                lines[d, b, r, 0:64, :] = volt[d, b, r, 0:8192].reshape(64, 128)
                lines[d, b, r, 64:72, :] = jnp.zeros((8, 128), F32)
                lines[d, b, r, 64:65, :] = volt[d, b, r, 8192:8320].reshape(1, 128)
                lines[d, b, r, 65:66, 0:96] = volt[d, b, r, 8320:8416].reshape(1, 96)

    lane = lax.broadcasted_iota(jnp.int32, (FINE, 128), 1)
    for b in range(2):
        for h in range(2):
            high_parts = []
            low_parts = []
            for r in range(2):
                for a in range(3):
                    block = jnp.concatenate([lines[4 * h + d, b, r, a:a + 64, :] for d in range(4)], axis=0)
                    high, low = split(block)
                    high_parts.append(high)
                    low_parts.append(low)
            window = jnp.concatenate(high_parts + low_parts + high_parts, axis=1)
            out = lax.dot_general(bank[...], window, NT, preferred_element_type=F32)
            for f in range(4):
                for p in range(2):
                    cols = slice(128 * p, 128 * p + 128)
                    first = out[f * 64:f * 64 + FINE, cols]
                    second = out[f * 64 + FINE:f * 64 + 2 * FINE, cols]
                    even = jnp.where(lane < 64, first, pltpu.roll(second, 64, 1))
                    odd = jnp.where(lane < 64, pltpu.roll(first, 64, 1), second)
                    at = b * 1024 + f * 8 + 4 * h + 2 * p
                    send[pl.ds(at, FINE, stride=32), :] = even
                    send[pl.ds(at + 1, FINE, stride=32), :] = odd

    slot = quad * 64 + chan

    def far(piece, lot):
        return pltpu.make_async_remote_copy(
            src_ref=phase_hbm.at[0, pl.ds(pl.multiple_of((1 - quad) * BEAMS + piece * 8, 8), 8)],
            dst_ref=phase_far.at[pl.ds(pl.multiple_of(piece * 8, 8), 8)],
            send_sem=far_send, recv_sem=far_recv.at[lot],
            device_id=(chan, 1 - quad), device_id_type=MESH)

    def far_lot(lot):
        rows = phase_far.at[pl.ds(LOTS[lot], LOTS[lot + 1] - LOTS[lot])]
        pltpu.make_async_copy(rows, rows, far_recv.at[lot]).wait()
        rows = pl.ds(LOTS[lot], LOTS[lot + 1] - LOTS[lot])
        gains(phase_far.at[rows], far_hi.at[rows], far_lo.at[rows])

    pl.semaphore_wait(barrier, PEERS - 1)
    for g, (start, stop) in enumerate(CHUNKS):
        count = 8 * (stop - start)

        def push(step, to_chan, to_quad):
            pltpu.make_async_remote_copy(
                src_ref=send.at[pl.ds(pl.multiple_of(to_chan * 32 + 8 * start, 8), count)],
                dst_ref=got.at[slot, pl.ds(8 * start, count)],
                send_sem=send_sem.at[g], recv_sem=recv_sem.at[g],
                device_id=(to_chan, to_quad), device_id_type=MESH).start()

        def between(step):
            if g == 0:
                lot = jnp.where(16 * step < LOTS[1], 0, 1)
                far(2 * step, lot).start()
                far(2 * step + 1, lot).start()

        each_peer(push, between)
    got[slot] = send[pl.ds(pl.multiple_of(chan * 32, 32), 32), :]

    own.wait()
    gains(phase_own, own_hi, own_lo)
    arrived(got, recv_sem.at[0], 0)
    prepare(got, (0, 1), quad, first_all, first_left)
    prepare(got, (2,), quad, both_all, second_left)

    def product_first(tile, carry):
        cols = pl.ds(pl.multiple_of(tile * 256, 256), 256)
        sums_ref[:, cols] = product([(first_left, first_all, 0, 2), (second_left, both_all, 0, 1)], cols)
        return carry

    lax.fori_loop(0, 4, product_first, 0)
    near = pl.ds(pl.multiple_of(quad * HALF, HALF), HALF)
    other = pl.ds(pl.multiple_of((1 - quad) * HALF, HALF), HALF)
    part = steered(own_hi, own_lo, first_all, near)

    def far_beams(lot):
        far_lot(lot)
        rows = slice(LOTS[lot], LOTS[lot + 1])
        powers = squared(part[rows] + steered(far_hi.at[rows], far_lo.at[rows], first_all, other))
        power_ref[rows] = side_by_side(powers[:, 0:128], powers[:, 128:256])

    far_beams(0)
    far_beams(1)
    arrived(got, recv_sem.at[1], 1)
    prepare(got, (3,), quad, both_all, left)
    for g in range(2):
        arrived(got, send_sem.at[g], g)
    pltpu.make_async_copy(phase_far, phase_far, far_send).wait()


def gains(source, high_ref, low_ref):
    for start in range(0, source.shape[0], 32):
        level = source[start:start + 32, :]
        for i in range(2):
            high, low = split(steer(level - 64 * i))
            high_ref[start:start + 32, i * HALF:i * HALF + HALF] = high
            low_ref[start:start + 32, i * HALF:i * HALF + HALF] = low


def arrived(got, sem, g):
    start, stop = CHUNKS[g]
    whole = got.at[pl.ds(0, PEERS - 1), pl.ds(8 * start, 8 * (stop - start))]
    pltpu.make_async_copy(whole, whole, sem).wait()


def prepare(got, parts, quad, everything, left):
    width = 128 * len(parts)
    lane = lax.broadcasted_iota(jnp.int32, (128, 128), 1)
    for i, f in enumerate(parts):
        col = 128 * (f % 2)
        for start in range(0, DISHES, 128):
            rows = slice(start, start + 128)
            block = got[start // 8:start // 8 + 16, 8 * f:8 * f + 8, :].reshape(128, 128)
            moved = pltpu.roll(block, 64, 1)
            high, low = split(block)
            everything[rows, col:col + 128] = high
            everything[rows, 256 + col:256 + col + 128] = low
            high, low = split(jnp.where(lane < 64, moved, -moved))
            everything[rows, 512 + col:512 + col + 128] = high
            everything[rows, 768 + col:768 + col + 128] = low
        for start in range(0, HALF, 128):
            rows = pl.ds(pl.multiple_of(quad * HALF + start, 128), 128)
            for turn in range(2):
                at = turn * HALF + start
                source = 512 * turn + col
                left[at:at + 128, 128 * i:128 * i + 128] = everything[rows, source:source + 128] * (1.0 / SPECTRA)
                left[at:at + 128, width + 128 * i:width + 128 * i + 128] = (
                    everything[rows, 256 + source:256 + source + 128] * (1.0 / SPECTRA))


def product(terms, cols):
    lhs = []
    rhs = []
    for left, everything, first, parts in terms:
        width = 128 * parts
        at = 128 * first
        high = left[:, 0:width]
        far_high = everything[cols, at:at + width]
        lhs += [high, high, left[:, width:2 * width]]
        rhs += [far_high, everything[cols, 256 + at:256 + at + width], far_high]
    return lax.dot_general(
        jnp.concatenate(lhs, axis=1), jnp.concatenate(rhs, axis=1), NT, preferred_element_type=F32)


def steered(gains_hi, gains_lo, everything, rows):
    both_high = jnp.concatenate([everything[rows, 0:256], everything[rows, 512:768]], axis=0)
    both_low = jnp.concatenate([everything[rows, 256:512], everything[rows, 768:1024]], axis=0)
    beams = jnp.dot(gains_hi[...], both_high, preferred_element_type=F32)
    beams += jnp.dot(gains_hi[...], both_low, preferred_element_type=F32)
    beams += jnp.dot(gains_lo[...], both_high, preferred_element_type=F32)
    return beams


def squared(beams):
    beams = beams * beams * (1.0 / DISHES)
    return jnp.concatenate(
        [beams[:, i:i + 128] + pltpu.roll(beams[:, i:i + 128], 64, 1) for i in (0, 128)], axis=1)


def side_by_side(first, second):
    lane = lax.broadcasted_iota(jnp.int32, first.shape, 1)
    return jnp.where(lane < 64, first, second)


def finish_kernel(sums_ref, left, everything, own_hi, own_lo, far_hi, far_lo, first_power, vis_hbm, power_hbm,
                  vis_ref, power_ref, vis_sem, power_sem):
    quad = lax.axis_index("quad")
    copies = []
    for tile in range(4):
        cols = pl.ds(tile * 256, 256)
        vis_ref[tile] = sums_ref[:, cols] + product([(left, everything, 1, 1)], cols)
        for i in range(2):
            copies.append(pltpu.make_async_copy(
                vis_ref.at[tile, pl.ds(i * HALF, HALF)], vis_hbm.at[0, i, :, cols], vis_sem.at[2 * tile + i]))
            copies[-1].start()

    near = pl.ds(pl.multiple_of(quad * HALF, HALF), HALF)
    other = pl.ds(pl.multiple_of((1 - quad) * HALF, HALF), HALF)
    powers = squared(steered(own_hi, own_lo, everything, near) + steered(far_hi, far_lo, everything, other))
    power = jnp.concatenate([first_power[...], side_by_side(powers[:, 0:128], powers[:, 128:256])], axis=1)
    source = lax.broadcasted_iota(jnp.int32, (SPECTRA, SPECTRA), 0)
    target = lax.broadcasted_iota(jnp.int32, (SPECTRA, SPECTRA), 1)
    order = (4 * (source % 64) + source // 64 == target).astype(BF16)
    high = power.astype(BF16)
    middle, low = split(power - high.astype(F32))
    power_ref[...] = (
        jnp.dot(high, order, preferred_element_type=F32)
        + jnp.dot(middle, order, preferred_element_type=F32)
        + jnp.dot(low, order, preferred_element_type=F32)
    )
    copy = pltpu.make_async_copy(power_ref, power_hbm.at[0], power_sem)
    copy.start()
    copy.wait()
    for copy in copies:
        copy.wait()


def per_device(voltages, filter_taps, phases):
    hbm_space = pl.BlockSpec(memory_space=pltpu.HBM)
    vmem_space = pl.BlockSpec(memory_space=VMEM)
    made = pl.pallas_call(
        spectra_kernel,
        name="spectra",
        out_shape=(
            jax.ShapeDtypeStruct((DISHES, DISHES), F32),
            jax.ShapeDtypeStruct((DISHES, 256), BF16),
            jax.ShapeDtypeStruct((DISHES, 1024), BF16),
            jax.ShapeDtypeStruct((BEAMS, DISHES), BF16),
            jax.ShapeDtypeStruct((BEAMS, DISHES), BF16),
            jax.ShapeDtypeStruct((BEAMS, DISHES), BF16),
            jax.ShapeDtypeStruct((BEAMS, DISHES), BF16),
            jax.ShapeDtypeStruct((BEAMS, 128), F32),
        ),
        in_specs=[hbm_space] * 3,
        out_specs=(vmem_space,) * 8,
        scratch_shapes=[
            VMEM((8, 2, 2, 8416), F32),
            VMEM((TAPS, FINE), F32),
            VMEM((8, 2, 2, 72, 128), F32),
            VMEM((256, 2304), BF16),
            VMEM((2048, 128), F32),
            VMEM((PEERS, 32, 128), F32),
            VMEM((DISHES, 1024), BF16),
            VMEM((DISHES, 512), BF16),
            VMEM((DISHES, 256), BF16),
            VMEM((BEAMS, HALF), jnp.int32),
            VMEM((BEAMS, HALF), jnp.int32),
            DMA,
            DMA,
            DMA((2,)),
            DMA((2,)),
            DMA,
            DMA,
            DMA((2,)),
        ],
        compiler_params=pltpu.CompilerParams(
            collective_id=0, has_side_effects=True, vmem_limit_bytes=28 * 2**20
        ),
    )(*[pltpu.with_memory_space_constraint(x, pltpu.HBM) for x in (voltages, filter_taps, phases)])
    return pl.pallas_call(
        finish_kernel,
        name="finish",
        out_shape=(
            jax.ShapeDtypeStruct((1, 2, HALF, DISHES), F32),
            jax.ShapeDtypeStruct((1, BEAMS, SPECTRA), F32),
        ),
        in_specs=[vmem_space] * 8,
        out_specs=(hbm_space, hbm_space),
        scratch_shapes=[VMEM((4, DISHES, 256), F32), VMEM((BEAMS, SPECTRA), F32), DMA((8,)), DMA],
        compiler_params=pltpu.CompilerParams(vmem_limit_bytes=16 * 2**20),
    )(*made)


def solution(mesh):
    return jax.shard_map(
        per_device,
        mesh=mesh,
        in_specs=(P("quad", "chan", None, None, None), P(), P("chan", None, "quad")),
        out_specs=(P("chan", None, "quad", None), P("chan", "quad", None)),
        check_vma=False,
    )
```
